128 devices in a mesh: dp: 16 (over x_lo, z, core), section: 8 (over y, x_hi).
Axes of the slice: x: 4 (x_hi: 2, x_lo: 2; x = x_hi * 2 + x_lo), y: 4, z: 4, core: 2. Of those that a mesh axis runs over, the one named last changes fastest.
Arguments:
- encoded: bfloat16 [16, 64, 2560], P('dp', 'section'), may hold values from -6 to 6
- source_len: int32 [16], replicated, may hold values from 16 to 64, as said below
- queries: bfloat16 [8, 16, 128, 8192], P('section', 'dp'), may hold values from -2.5 to 2.5
- saved_keys: bfloat16 [8, 16, 64, 8192], P('section', 'dp'), may hold values from -2.5 to 2.5
- saved_values: bfloat16 [8, 16, 64, 8192], P('section', 'dp'), may hold values from -6 to 6
- out_grad: bfloat16 [8, 16, 128, 8192], P('section', 'dp'), may hold values from -6 to 6
- key_weight: bfloat16 [8, 2560, 8192], P('section', None, 'dp'), may hold values from -0.0625 to 0.0625
- value_weight: bfloat16 [8, 2560, 8192], P('section', None, 'dp'), may hold values from -0.0625 to 0.0625
Outputs:
- encoder_grad: float32 [16, 64, 2560], P('dp', 'section')
- key_update: float32 [8, 2560, 8192], P('section', None, 'dp')
- value_update: float32 [8, 2560, 8192], P('section', None, 'dp')
The draws below stay inside these ranges and needn't reach their ends.
Inputs may be any that keep to these rules, and one draw needn't show every extreme that they name: `source_len`: some sample has no padding.
All inputs are finite; a program needn't handle non-finite values.
Results may differ from the reference program's by a relative error of at most 0.0063.
Values may be sent and summed in bfloat16 or wider, within the bound.
No kernel may reach another device: no remote copies, remote signals or barrier semaphores. Data moves between devices by JAX's collectives and lax.ppermute only.
A program may use at most 128 MiB of HBM per device.

```python
import math
import jax
import jax.numpy as jnp
from jax import lax

D = 2560
HEADS = 64
HEAD = 128
SWEEPS = 5
TGT = 128
SRC = 64
INNER = 8192
SAMPLES = 16
LAYERS = 8


def draw_source_len(key, part):
    key = jax.random.fold_in(key, 5)
    first_key, second_key = jax.random.split(key)
    lengths = jax.random.randint(first_key, (SAMPLES,), SRC // 4, SRC + 1)
    chosen = jax.random.randint(second_key, (), 0, SAMPLES)
    return jnp.where(jnp.arange(SAMPLES) == chosen, SRC, lengths).astype(jnp.int32)


def level_of(own_key, dims, cuts, smallest, top_value):
    gain = 1.0
    for dim, shards_of in cuts:
        steps = jax.random.uniform(jax.random.fold_in(jax.random.fold_in(own_key, 6), dim), (shards_of,), jnp.float32, smallest / len(cuts), top_value / len(cuts))
        gain = gain * jnp.repeat(jnp.exp(steps), dims[dim] // shards_of).reshape((-1,) + (1,) * (len(dims) - 1 - dim))
    return gain


def centred(key, shape, spread, bound, cuts=(), held_as=jnp.bfloat16):
    loudness = level_of(key, shape, cuts, -0.22, 0.18) if cuts else 1.0
    drawn = jax.random.normal(key, shape, jnp.float32) * spread * loudness
    return jnp.minimum(jnp.maximum(drawn, -bound), bound).astype(held_as)


def setup_inputs(seed: int = 0) -> dict:
    key_list = jax.random.split(jax.random.key(seed), 9)
    return {
        "encoded": centred(key_list[0], (SAMPLES, SRC, D), 1.0, 6.0, ((0, 16), (1, 8))),
        "source_len": draw_source_len(jax.random.fold_in(key_list[8], 71), 0),
        "queries": centred(key_list[2], (LAYERS, SAMPLES, TGT, INNER), 1.0, 2.5, ((0, 8), (1, 16))),
        "saved_keys": centred(key_list[3], (LAYERS, SAMPLES, SRC, INNER), 1.0, 2.5, ((0, 8), (1, 16))),
        "saved_values": centred(key_list[4], (LAYERS, SAMPLES, SRC, INNER), 1.0, 6.0, ((0, 8), (1, 16))),
        "out_grad": centred(key_list[5], (LAYERS, SAMPLES, TGT, INNER), 1.0, 6.0, ((0, 8), (1, 16))),
        "key_weight": centred(key_list[6], (LAYERS, D, INNER), INNER ** -0.5, 0.0625, ((0, 8), (2, 16))),
        "value_weight": centred(key_list[7], (LAYERS, D, INNER), INNER ** -0.5, 0.0625, ((0, 8), (2, 16))),
    }


LINEAR_COEFF = 3.4445
SQUARE_COEFF = -4.775
CUBIC_COEFF = 2.0315

def orthogonalize(gradient):
    norms = jnp.sqrt(lax.optimization_barrier(jnp.sum(gradient * gradient, axis=(0, 2), keepdims=True))) + 1e-07
    current = gradient / norms
    for sweep in range(SWEEPS):
        gram = jnp.einsum('dhi,dhj->hij', current, current, precision=lax.Precision.HIGHEST)
        squared = jnp.einsum('hij,hjk->hik', gram, gram, precision=lax.Precision.HIGHEST)
        mixer = SQUARE_COEFF * gram + CUBIC_COEFF * squared
        current = LINEAR_COEFF * current + jnp.einsum('dhi,hij->dhj', current, mixer, precision=lax.Precision.HIGHEST)
    return current * math.sqrt(D)

def attention_grads(query_part, key_part, value_part, grad_part, valid):
    samples, tgt_rows, width = query_part.shape
    src_rows = key_part.shape[1]
    heads = width // HEAD
    query_four = query_part.reshape(samples, tgt_rows, heads, HEAD).astype(jnp.float32)
    key_four = key_part.reshape(samples, src_rows, heads, HEAD).astype(jnp.float32)
    value_four = value_part.reshape(samples, src_rows, heads, HEAD).astype(jnp.float32)
    grad_four = grad_part.reshape(samples, tgt_rows, heads, HEAD).astype(jnp.float32)
    scale = 1.0 / math.sqrt(HEAD)
    scores = jnp.einsum('bthe,bshe->bhts', query_four, key_four) * scale
    weights_raw = jnp.exp(scores) * valid[:, None, None, :]
    probs = weights_raw / lax.optimization_barrier(jnp.sum(weights_raw, axis=-1, keepdims=True))
    probs_low = probs.astype(jnp.bfloat16).astype(jnp.float32)
    grad_values = jnp.einsum('bhts,bthe->bshe', probs_low, grad_four).astype(jnp.bfloat16)
    grad_probs = jnp.einsum('bthe,bshe->bhts', grad_four, value_four)
    delta = lax.optimization_barrier(jnp.sum(probs * grad_probs, axis=-1, keepdims=True))
    grad_scores = (probs * (grad_probs - delta) * scale).astype(jnp.bfloat16).astype(jnp.float32)
    grad_keys = jnp.einsum('bhts,bthe->bshe', grad_scores, query_four).astype(jnp.bfloat16)
    return (grad_keys.reshape(samples, src_rows, width), grad_values.reshape(samples, src_rows, width))

def reference(encoded, source_len, queries, saved_keys, saved_values, out_grad, key_weight, value_weight):
    valid = (jnp.arange(SRC, dtype=jnp.int32)[None, :] < source_len[:, None]).astype(jnp.float32)
    enc_rows = encoded.reshape(SAMPLES * SRC, D)

    def one_layer(total, inputs):
        layer_queries, layer_keys, layer_values, layer_grads, layer_kw, layer_vw = inputs
        grad_keys, grad_values = attention_grads(layer_queries, layer_keys, layer_values, layer_grads, valid)
        key_rows = grad_keys.reshape(SAMPLES * SRC, INNER)
        value_rows = grad_values.reshape(SAMPLES * SRC, INNER)
        total = total + jnp.dot(key_rows, layer_kw.T, preferred_element_type=jnp.float32)
        total = total + jnp.dot(value_rows, layer_vw.T, preferred_element_type=jnp.float32)
        key_sum = jnp.dot(enc_rows.T, key_rows, preferred_element_type=jnp.float32)
        value_sum = jnp.dot(enc_rows.T, value_rows, preferred_element_type=jnp.float32)
        stacked = jnp.concatenate([key_sum.reshape(D, HEADS, HEAD), value_sum.reshape(D, HEADS, HEAD)], axis=1)
        result = orthogonalize(stacked)
        key_update = result[:, :HEADS].reshape(D, INNER)
        value_update = result[:, HEADS:].reshape(D, INNER)
        return (total, (key_update, value_update))
    total, updates = lax.scan(one_layer, jnp.zeros((SAMPLES * SRC, D), jnp.float32), (queries, saved_keys, saved_values, out_grad, key_weight, value_weight))
    encoder_grad = total.reshape(SAMPLES, SRC, D)
    return (encoder_grad, updates[0], updates[1])
```

```python
import functools
import math

import jax
import jax.numpy as jnp
from jax import lax
from jax.experimental import pallas as pl
from jax.experimental.pallas import tpu as pltpu
from jax.sharding import Mesh, PartitionSpec as P

D = 2560
HEAD = 128
SWEEPS = 5

LINEAR_COEFF = 3.4445
SQUARE_COEFF = -4.775
CUBIC_COEFF = 2.0315

BF16 = jnp.bfloat16
F32 = jnp.float32
HIGHEST = lax.Precision.HIGHEST

MIB = 1024 * 1024


def dot(a, b, dims, precision=None):
    return lax.dot_general(a, b, (dims, ((), ())), precision=precision, preferred_element_type=F32)


def attention_kernel(place, lens, q_ref, k_ref, v_ref, g_ref, out_ref):
    src = k_ref.shape[0]
    tgt = q_ref.shape[0]
    heads = q_ref.shape[1] // HEAD
    row = lax.broadcasted_iota(jnp.int32, (src, tgt), 0)
    valid = (row < lens[place[0]]).astype(F32)
    scale = 1.0 / math.sqrt(HEAD)
    width = heads * HEAD
    cols = [slice(h * HEAD, (h + 1) * HEAD) for h in range(heads)]
    cat = jnp.concatenate
    both = [
        dot(cat([k_ref[:, c], v_ref[:, c]], 0), cat([q_ref[:, c], g_ref[:, c]], 0), ((1,), (1,))) for c in cols
    ]
    grad_probs = [b[src:, tgt:] for b in both]
    raw = [jnp.exp2(b[:src, :tgt] * (scale * math.log2(math.e))) * valid for b in both]
    probs = [r * (1.0 / jnp.sum(r, axis=0, keepdims=True)) for r in raw]
    delta = [jnp.sum(p * g, axis=0, keepdims=True) for p, g in zip(probs, grad_probs)]
    low = [
        cat([(p * ((g - d) * scale)).astype(BF16), p.astype(BF16)], 0)
        for p, g, d in zip(probs, grad_probs, delta)
    ]
    for h, c in enumerate(cols):
        grads = dot(low[h], cat([q_ref[:, c], g_ref[:, c]], 1), ((1,), (0,)))
        out_ref[:, c] = grads[:src, :HEAD].astype(BF16)
        out_ref[:, width + h * HEAD : width + (h + 1) * HEAD] = grads[src:, HEAD:].astype(BF16)


def attention(place, lens, q, k, v, g, chips, group):
    tgt, src = q.shape[0], k.shape[0]

    def col(p, r, place, lens):
        return (0, 2 * p + lax.bitwise_xor(lax.rem(place[0], 2), r))

    return pl.pallas_call(
        attention_kernel,
        grid_spec=pltpu.PrefetchScalarGridSpec(
            num_scalar_prefetch=2,
            grid=(chips, 2),
            in_specs=[
                pl.BlockSpec((tgt, group), col),
                pl.BlockSpec((src, group), col),
                pl.BlockSpec((src, group), col),
                pl.BlockSpec((tgt, group), col),
            ],
            out_specs=pl.BlockSpec((None, src, 2 * group), lambda p, r, place, lens: (p, 0, r)),
        ),
        out_shape=jax.ShapeDtypeStruct((chips, src, 4 * group), BF16),
        compiler_params=pltpu.CompilerParams(vmem_limit_bytes=56 * MIB),
        cost_estimate=pl.CostEstimate(flops=700_000_000, bytes_accessed=8 * MIB, transcendentals=600_000),
        name="attention",
    )(place, lens, q, k, v, g)


def partial_kernel(kv_ref, kw_ref, vw_ref, okw_ref, ovw_ref, out_ref):
    w = kw_ref.shape[1]
    total = None
    for i, ref in enumerate((kw_ref, vw_ref, okw_ref, ovw_ref)):
        term = dot(kv_ref[:, i * w : (i + 1) * w], ref[...], ((1,), (1,)))
        total = term if total is None else total + term
    out_ref[...] = total.astype(BF16)


def encoder_partial(kv, kw, vw, okw, ovw):
    rows, feats = kv.shape
    width, w = kw.shape
    tile = 512
    spec = pl.BlockSpec((tile, w), lambda j: (j, 0))
    return pl.pallas_call(
        partial_kernel,
        grid=(width // tile,),
        in_specs=[pl.BlockSpec((rows, feats), lambda j: (0, 0)), spec, spec, spec, spec],
        out_specs=pl.BlockSpec((rows, tile), lambda j: (0, j)),
        out_shape=jax.ShapeDtypeStruct((rows, width), BF16),
        compiler_params=pltpu.CompilerParams(vmem_limit_bytes=56 * MIB),
        cost_estimate=pl.CostEstimate(
            flops=2 * rows * feats * width, bytes_accessed=16 * MIB, transcendentals=0
        ),
        name="encoder_partial",
    )(kv, kw, vw, okw, ovw)


def two_parts(x):
    high = x.astype(BF16)
    low = (x - high.astype(F32)).astype(BF16)
    return high, low


def update_kernel(pairs, e_ref, oe_ref, kv_ref, okv_ref, key_ref, value_ref, parts, gram, mix):
    step = pl.program_id(0)
    width = e_ref.shape[1]
    heads = 2 * pairs

    @pl.when(step < pairs)
    def _():
        total = dot(kv_ref[...], e_ref[...], ((0,), (0,))) + dot(okv_ref[...], oe_ref[...], ((0,), (0,)))
        for h in range(2):
            high, low = two_parts(total[h * HEAD : (h + 1) * HEAD])
            both = jnp.concatenate([high, low], axis=0)
            parts[2 * step + h] = both
            full = dot(both, both, ((1,), (1,)))
            gram[2 * step + h] = (full[:HEAD, :HEAD] + full[HEAD:, HEAD:]) + (
                full[:HEAD, HEAD:] + full[HEAD:, :HEAD]
            )

    @pl.when(step == pairs)
    def _():
        row = lax.broadcasted_iota(jnp.int32, (HEAD, HEAD), 0)
        eye = (row == lax.broadcasted_iota(jnp.int32, (HEAD, HEAD), 1)).astype(F32)

        def prod(a, b):
            return dot(a, b, ((1,), (0,)), HIGHEST)

        for h in range(heads):
            whole = gram[h]
            trace = jnp.sum(jnp.sum(whole * eye, axis=1, keepdims=True), axis=0, keepdims=True)
            inverse = 1.0 / (jnp.sqrt(trace) + 1e-07)
            gram[h] = whole * inverse * inverse
            mix[h] = eye * (inverse * math.sqrt(width))

        def sweep(_, carry):
            grams = [gram[h] for h in range(heads)]
            squares = [prod(a, a) for a in grams]
            steps = [
                LINEAR_COEFF * eye + (SQUARE_COEFF * a + CUBIC_COEFF * s) for a, s in zip(grams, squares)
            ]
            halves = [prod(a, m) for a, m in zip(grams, steps)]
            mixes = [prod(mix[h], m) for h, m in enumerate(steps)]
            nexts = [prod(m, a) for a, m in zip(halves, steps)]
            for h in range(heads):
                gram[h] = nexts[h]
                mix[h] = mixes[h]
            return carry

        lax.fori_loop(0, SWEEPS, sweep, 0)

    def finish(ref):
        first = 2 * (step - pairs - 1)
        for h in range(2):
            high, low = two_parts(mix[first + h])
            line = jnp.concatenate([high, low], axis=1)
            right = jnp.concatenate([line, line], axis=0)
            out = dot(parts[first + h], right, ((0,), (0,)))
            ref[:, h * HEAD : (h + 1) * HEAD] = out[:, :HEAD] + out[:, HEAD:]

    @pl.when(jnp.logical_and(step > pairs, step <= pairs + pairs // 2))
    def _():
        finish(key_ref)

    @pl.when(step > pairs + pairs // 2)
    def _():
        finish(value_ref)


def updates(e, oe, kv, okv, inner):
    rows, width = e.shape
    heads = 2 * inner // HEAD
    pairs = heads // 2
    half = pairs // 2
    wide = 2 * HEAD
    whole = pl.BlockSpec((rows, width), lambda i: (0, 0))
    cols = pl.BlockSpec((rows, wide), lambda i: (0, jnp.minimum(i, pairs - 1)))
    return pl.pallas_call(
        functools.partial(update_kernel, pairs),
        grid=(2 * pairs + 1,),
        in_specs=[whole, whole, cols, cols],
        out_specs=[
            pl.BlockSpec((width, wide), lambda i: (0, jnp.clip(i - pairs - 1, 0, half - 1))),
            pl.BlockSpec((width, wide), lambda i: (0, jnp.clip(i - pairs - 1 - half, 0, half - 1))),
        ],
        out_shape=[jax.ShapeDtypeStruct((width, inner), F32)] * 2,
        scratch_shapes=[
            pltpu.VMEM((heads, 2 * HEAD, width), BF16),
            pltpu.VMEM((heads, HEAD, HEAD), F32),
            pltpu.VMEM((heads, HEAD, HEAD), F32),
        ],
        compiler_params=pltpu.CompilerParams(vmem_limit_bytes=56 * MIB),
        cost_estimate=pl.CostEstimate(
            flops=20_000_000_000, bytes_accessed=20 * MIB, transcendentals=0
        ),
        name="updates",
    )(e, oe, kv, okv)


def ring(size, shift):
    return [(j, (j + shift) % size) for j in range(size)]


def gather_ring(block, axis, size, dim):
    own = lax.axis_index(axis)
    got = [(0, block)]
    for shift in ((2, 1, 3) if size == 4 else range(1, size)):
        got.append((shift, lax.ppermute(block, axis, ring(size, shift))))
    shape = block.shape[:dim] + (size,) + block.shape[dim:]
    out = jnp.zeros(shape, block.dtype)
    for shift, piece in got:
        out = lax.dynamic_update_index_in_dim(out, piece, lax.rem(own - shift + size, size), dim)
    return out


def body(
    encoded, source_len, queries, saved_keys, saved_values, out_grad, key_weight, value_weight
):
    across = [(0, 1), (1, 0)]
    key_weight, value_weight = key_weight[0], value_weight[0]
    width, inner = key_weight.shape
    block = encoded.shape[1]

    spread = jnp.broadcast_to(encoded, (16, block, width))
    near = lax.all_to_all(spread, ("xl", "z", "xh"), split_axis=0, concat_axis=0, tiled=True)

    place = lax.axis_index(("xl", "z", "c")).astype(jnp.int32).reshape(1)
    local = attention(
        place, source_len, queries[0, 0], saved_keys[0, 0], saved_values[0, 0], out_grad[0, 0], 8, inner
    )
    moved = lax.all_to_all(local, ("xl", "z"), split_axis=0, concat_axis=0, tiled=True)
    rows = moved.reshape(8 * local.shape[1], 4 * inner)

    near, key_send, value_send, _ = lax.optimization_barrier((near, key_weight, value_weight, local))
    own_rows = gather_ring(near.reshape(8, 2 * block, width), "y", 4, 1).reshape(64 * block, width)
    other_kw = lax.ppermute(key_send, "c", across)
    other_vw = lax.ppermute(value_send, "c", across)
    other_rows = lax.ppermute(own_rows, "c", across)

    partial = encoder_partial(rows, key_weight, value_weight, other_kw, other_vw)
    terms = lax.all_to_all(partial, ("xl", "z", "y", "xh"), split_axis=0, concat_axis=0, tiled=True)
    held, _ = lax.optimization_barrier((rows, partial))
    other_kv = lax.ppermute(held[:, 2 * inner :], "c", across)
    key_update, value_update = updates(own_rows, other_rows, held, other_kv, inner)
    encoder_grad = jnp.sum(terms.reshape(64, block, width).astype(F32), axis=0)
    return encoder_grad[None], key_update[None], value_update[None]


def solution(mesh):
    fine = Mesh(mesh.devices.reshape(2, 4, 2, 4, 2), ("xl", "z", "c", "y", "xh"))
    dp, section = ("xl", "z", "c"), ("y", "xh")
    in_specs = (
        P(dp, section, None),
        P(),
        P(section, dp, None, None),
        P(section, dp, None, None),
        P(section, dp, None, None),
        P(section, dp, None, None),
        P(section, None, dp),
        P(section, None, dp),
    )
    out_specs = (P(dp, section, None), P(section, None, dp), P(section, None, dp))
    return jax.shard_map(body, mesh=fine, in_specs=in_specs, out_specs=out_specs, check_vma=False)
```

```python
import functools
import math

import jax
import jax.numpy as jnp
from jax import lax
from jax.experimental import pallas as pl
from jax.experimental.pallas import tpu as pltpu
from jax.sharding import Mesh, PartitionSpec as P

D = 2560
HEAD = 128
SWEEPS = 5

LINEAR_COEFF = 3.4445
SQUARE_COEFF = -4.775
CUBIC_COEFF = 2.0315

BF16 = jnp.bfloat16
F32 = jnp.float32
HIGHEST = lax.Precision.HIGHEST

MIB = 1024 * 1024


def dot(a, b, dims, precision=None):
    return lax.dot_general(a, b, (dims, ((), ())), precision=precision, preferred_element_type=F32)


def attention_kernel(place, lens, q_ref, k_ref, v_ref, g_ref, out_ref):
    src = k_ref.shape[0]
    tgt = q_ref.shape[0]
    group = out_ref.shape[2] // 4
    core = lax.rem(place[0], 2)
    row = lax.broadcasted_iota(jnp.int32, (src, tgt), 0)
    valid = (row < lens[place[0]]).astype(F32)
    scale = 1.0 / math.sqrt(HEAD)
    cols = [slice(h * HEAD, (h + 1) * HEAD) for h in range(q_ref.shape[1] // HEAD)]
    cat = jnp.concatenate
    both = [
        dot(cat([k_ref[:, c], v_ref[:, c]], 0), cat([q_ref[:, c], g_ref[:, c]], 0), ((1,), (1,))) for c in cols
    ]
    grad_probs = [b[src:, tgt:] for b in both]
    raw = [jnp.exp2(b[:src, :tgt] * (scale * math.log2(math.e))) * valid for b in both]
    probs = [r * (1.0 / jnp.sum(r, axis=0, keepdims=True)) for r in raw]
    delta = [jnp.sum(p * g, axis=0, keepdims=True) for p, g in zip(probs, grad_probs)]
    low = [
        cat([(p * ((g - d) * scale)).astype(BF16), p.astype(BF16)], 0)
        for p, g, d in zip(probs, grad_probs, delta)
    ]
    for h, c in enumerate(cols):
        grads = dot(low[h], cat([q_ref[:, c], g_ref[:, c]], 1), ((1,), (0,)))
        chip, of_core, at = h * HEAD // (2 * group), h * HEAD // group % 2, h * HEAD % group
        first = lax.bitwise_xor(core, of_core) * 2 * group + at
        out_ref[chip, :, pl.ds(pl.multiple_of(first, HEAD), HEAD)] = grads[:src, :HEAD].astype(BF16)
        out_ref[chip, :, pl.ds(pl.multiple_of(first + group, HEAD), HEAD)] = grads[src:, HEAD:].astype(BF16)


def attention(place, lens, q, k, v, g, chips, group):
    tgt, src = q.shape[0], k.shape[0]
    some = 2
    wide = 2 * group * some

    def col(p, place, lens):
        return (0, p)

    return pl.pallas_call(
        attention_kernel,
        grid_spec=pltpu.PrefetchScalarGridSpec(
            num_scalar_prefetch=2,
            grid=(chips // some,),
            in_specs=[
                pl.BlockSpec((tgt, wide), col),
                pl.BlockSpec((src, wide), col),
                pl.BlockSpec((src, wide), col),
                pl.BlockSpec((tgt, wide), col),
            ],
            out_specs=pl.BlockSpec((some, src, 4 * group), lambda p, place, lens: (p, 0, 0)),
        ),
        out_shape=jax.ShapeDtypeStruct((chips, src, 4 * group), BF16),
        compiler_params=pltpu.CompilerParams(vmem_limit_bytes=56 * MIB),
        cost_estimate=pl.CostEstimate(flops=700_000_000, bytes_accessed=8 * MIB, transcendentals=600_000),
        name="attention",
    )(place, lens, q, k, v, g)


def partial_kernel(kv_ref, kw_ref, vw_ref, okw_ref, ovw_ref, out_ref):
    w = kw_ref.shape[1]
    total = None
    for i, ref in enumerate((kw_ref, vw_ref, okw_ref, ovw_ref)):
        term = dot(kv_ref[:, i * w : (i + 1) * w], ref[...], ((1,), (1,)))
        total = term if total is None else total + term
    out_ref[...] = total.astype(BF16)


def encoder_partial(kv, kw, vw, okw, ovw):
    rows, feats = kv.shape
    width, w = kw.shape
    tile = 512
    spec = pl.BlockSpec((tile, w), lambda j: (j, 0))
    return pl.pallas_call(
        partial_kernel,
        grid=(width // tile,),
        in_specs=[pl.BlockSpec((rows, feats), lambda j: (0, 0)), spec, spec, spec, spec],
        out_specs=pl.BlockSpec((rows, tile), lambda j: (0, j)),
        out_shape=jax.ShapeDtypeStruct((rows, width), BF16),
        compiler_params=pltpu.CompilerParams(vmem_limit_bytes=56 * MIB),
        cost_estimate=pl.CostEstimate(
            flops=2 * rows * feats * width, bytes_accessed=16 * MIB, transcendentals=0
        ),
        name="encoder_partial",
    )(kv, kw, vw, okw, ovw)


def two_parts(x):
    high = x.astype(BF16)
    low = (x - high.astype(F32)).astype(BF16)
    return high, low


def update_kernel(y_shifts, spot, *refs):
    count = 2 * len(y_shifts)
    pieces, rest = refs[:count], refs[count:]
    kv_ref, okv_ref, key_ref, value_ref, lines, parts, gram, mix, result, sems = rest
    width = pieces[0].shape[1]
    inner = key_ref.shape[1]
    heads = inner // HEAD
    chunk = inner
    chunks = width // chunk

    row = lax.broadcasted_iota(jnp.int32, (HEAD, HEAD), 0)
    eye = (row == lax.broadcasted_iota(jnp.int32, (HEAD, HEAD), 1)).astype(F32)

    def prod(a, b):
        return dot(a, b, ((1,), (0,)), HIGHEST)

    def near_prod(a, b):
        left = jnp.concatenate(two_parts(a), axis=1)
        line = jnp.concatenate(two_parts(b), axis=1)
        full = dot(left, jnp.concatenate([line, line], axis=0), ((1,), (0,)))
        return full[:, :HEAD] + full[:, HEAD:]

    at = 0
    for ref in (kv_ref, okv_ref):
        for y in y_shifts:
            some = ref[:, lax.rem(spot[0] + (4 - y), 4)]
            some = some.reshape(-1, some.shape[2])
            lines[:, at : at + some.shape[0]] = some.T
            at += some.shape[0]

    def lanes(i):
        return slice(i * chunk, (i + 1) * chunk)

    def sums(first, i):
        rows = jnp.concatenate([ref[:, lanes(i)] for ref in pieces], axis=0)
        total = dot(lines[first * HEAD : (first + heads) * HEAD], rows, ((1,), (0,)))
        for h in range(heads):
            both = jnp.concatenate(two_parts(total[h * HEAD : (h + 1) * HEAD]), axis=0)
            parts[first + h, :, lanes(i)] = both
            full = dot(both, both, ((1,), (1,)))
            term = (full[:HEAD, :HEAD] + full[HEAD:, HEAD:]) + (full[:HEAD, HEAD:] + full[HEAD:, :HEAD])
            gram[first + h] = gram[first + h] + term

    def start(first):
        for h in range(first, first + heads):
            whole = gram[h]
            trace = jnp.sum(jnp.sum(whole * eye, axis=1, keepdims=True), axis=0, keepdims=True)
            inverse = 1.0 / (jnp.sqrt(trace) + 1e-07)
            gram[h] = whole * inverse * inverse
            mix[h] = eye * (inverse * math.sqrt(width))

    def sweep(first, last):
        grams = [gram[first + h] for h in range(heads)]
        squares = [near_prod(a, a) for a in grams]
        steps = [LINEAR_COEFF * eye + (SQUARE_COEFF * a + CUBIC_COEFF * s) for a, s in zip(grams, squares)]
        mixes = [near_prod(mix[first + h], m) for h, m in enumerate(steps)]
        for h in range(heads):
            mix[first + h] = mixes[h]
        if not last:
            halves = [prod(a, m) for a, m in zip(grams, steps)]
            nexts = [prod(m, a) for a, m in zip(halves, steps)]
            for h in range(heads):
                gram[first + h] = nexts[h]

    def leave(first, i, ref):
        rows = lanes(i)
        place = 0 if first == 0 else 1
        return pltpu.make_async_copy(result.at[place, rows], ref.at[rows], sems.at[place, i])

    def finish(first, i, ref):
        place = 0 if first == 0 else 1
        for h in range(heads):
            line = jnp.concatenate(two_parts(mix[first + h]), axis=1)
            right = jnp.concatenate([line, line], axis=0)
            out = dot(parts[first + h, :, lanes(i)], right, ((0,), (0,)))
            result[place, lanes(i), h * HEAD : (h + 1) * HEAD] = out[:, :HEAD] + out[:, HEAD:]
        leave(first, i, ref).start()

    gram[...] = jnp.zeros_like(gram)

    for i in range(chunks):
        sums(0, i)
    start(0)
    for i in range(SWEEPS):
        sums(heads, i)
        sweep(0, i == SWEEPS - 1)
    start(heads)
    for i in range(SWEEPS):
        finish(0, i, key_ref)
        sweep(heads, i == SWEEPS - 1)
    for i in range(chunks):
        finish(heads, i, value_ref)
    for i in range(chunks):
        leave(0, i, key_ref).wait()
        leave(heads, i, value_ref).wait()


def updates(spot, y_shifts, pieces, kv, okv, inner):
    rows, width = pieces[0].shape
    blocks, size, block = kv.shape[:3]
    heads = 2 * inner // HEAD
    chunks = width // inner
    assert chunks == SWEEPS
    whole = pl.BlockSpec((rows, width), lambda i, spot: (0, 0))

    def half(at):
        return pl.BlockSpec((blocks, size, block, 2 * inner), lambda i, spot: (0, 0, 0, at))

    return pl.pallas_call(
        functools.partial(update_kernel, y_shifts),
        grid_spec=pltpu.PrefetchScalarGridSpec(
            num_scalar_prefetch=1,
            grid=(1,),
            in_specs=[whole] * len(pieces) + [half(0), half(1)],
            out_specs=[pl.BlockSpec(memory_space=pl.ANY)] * 2,
            scratch_shapes=[
                pltpu.VMEM((2 * inner, 2 * blocks * size * block), BF16),
                pltpu.VMEM((heads, 2 * HEAD, width), BF16),
                pltpu.VMEM((heads, HEAD, HEAD), F32),
                pltpu.VMEM((heads, HEAD, HEAD), F32),
                pltpu.VMEM((2, width, inner), F32),
                pltpu.SemaphoreType.DMA((2, chunks)),
            ],
        ),
        out_shape=[jax.ShapeDtypeStruct((width, inner), F32)] * 2,
        compiler_params=pltpu.CompilerParams(vmem_limit_bytes=56 * MIB),
        cost_estimate=pl.CostEstimate(
            flops=20_000_000_000, bytes_accessed=20 * MIB, transcendentals=0
        ),
        name="updates",
    )(spot, *pieces, kv, okv)


def ring(shift):
    return [(j, (j + shift) % 4) for j in range(4)]


def body(
    encoded, source_len, queries, saved_keys, saved_values, out_grad, key_weight, value_weight
):
    across = [(0, 1), (1, 0)]
    key_weight, value_weight = key_weight[0], value_weight[0]
    width, inner = key_weight.shape
    block = encoded.shape[1]

    spread = jnp.broadcast_to(encoded, (16, block, width))
    near = lax.all_to_all(spread, ("xl", "z", "xh"), split_axis=0, concat_axis=0, tiled=True)
    near = near.reshape(16 * block, width)

    place = lax.axis_index(("xl", "z", "c")).astype(jnp.int32).reshape(1)
    local = attention(
        place, source_len, queries[0, 0], saved_keys[0, 0], saved_values[0, 0], out_grad[0, 0], 8, inner
    )
    moved = lax.all_to_all(local, ("xl", "z"), split_axis=0, concat_axis=0, tiled=True)

    near, key_send, value_send, _ = lax.optimization_barrier((near, key_weight, value_weight, local))
    shifts = (0, 2, 1, 3)
    own_rows = [near] + [lax.ppermute(near, "y", ring(s)) for s in shifts[1:]]
    other_kw = lax.ppermute(key_send, "c", across)
    other_vw = lax.ppermute(value_send, "c", across)

    moved, own_rows[2], own_rows[3] = lax.optimization_barrier((moved, own_rows[2], own_rows[3]))
    rows = moved.reshape(8 * local.shape[1], 4 * inner)
    other_rows = [lax.ppermute(r, "c", across) for r in own_rows]
    other_moved = lax.ppermute(moved, "c", across)
    partial = encoder_partial(rows, key_weight, value_weight, other_kw, other_vw)
    terms = lax.all_to_all(
        partial, ("xl", "z", "y", "xh"), split_axis=0, concat_axis=0, tiled=True
    )

    spot = lax.axis_index("y").astype(jnp.int32).reshape(1)
    by_y = (8, 4, 2 * block, 4 * inner)
    key_update, value_update = updates(
        spot, shifts, own_rows + other_rows, moved.reshape(by_y), other_moved.reshape(by_y), inner
    )
    encoder_grad = jnp.sum(terms.reshape(64, block, width).astype(F32), axis=0)
    return encoder_grad[None], key_update[None], value_update[None]


def solution(mesh):
    fine = Mesh(mesh.devices.reshape(2, 4, 2, 4, 2), ("xl", "z", "c", "y", "xh"))
    dp, section = ("xl", "z", "c"), ("y", "xh")
    in_specs = (
        P(dp, section, None),
        P(),
        P(section, dp, None, None),
        P(section, dp, None, None),
        P(section, dp, None, None),
        P(section, dp, None, None),
        P(section, None, dp),
        P(section, None, dp),
    )
    out_specs = (P(dp, section, None), P(section, None, dp), P(section, None, dp))
    return jax.shard_map(body, mesh=fine, in_specs=in_specs, out_specs=out_specs, check_vma=False)
```

```python
import functools
import math

import jax
import jax.numpy as jnp
from jax import lax
from jax.experimental import pallas as pl
from jax.experimental.pallas import tpu as pltpu
from jax.sharding import Mesh, PartitionSpec as P

D = 2560
HEAD = 128
SWEEPS = 5

LINEAR_COEFF = 3.4445
SQUARE_COEFF = -4.775
CUBIC_COEFF = 2.0315

BF16 = jnp.bfloat16
F32 = jnp.float32
HIGHEST = lax.Precision.HIGHEST

MIB = 1024 * 1024


def dot(a, b, dims, precision=None):
    return lax.dot_general(a, b, (dims, ((), ())), precision=precision, preferred_element_type=F32)


def attention_kernel(place, lens, q_ref, k_ref, v_ref, g_ref, *refs):
    out_ref = refs[-1]
    src = k_ref.shape[0]
    tgt = q_ref.shape[0]
    group = out_ref.shape[2] // 4
    core = lax.rem(place[0], 2)
    row = lax.broadcasted_iota(jnp.int32, (src, tgt), 0)
    valid = (row < lens[place[0]]).astype(F32)
    scale = 1.0 / math.sqrt(HEAD)
    cols = [slice(h * HEAD, (h + 1) * HEAD) for h in range(q_ref.shape[1] // HEAD)]
    cat = jnp.concatenate
    both = [
        dot(cat([k_ref[:, c], v_ref[:, c]], 0), cat([q_ref[:, c], g_ref[:, c]], 0), ((1,), (1,))) for c in cols
    ]
    grad_probs = [b[src:, tgt:] for b in both]
    raw = [jnp.exp2(b[:src, :tgt] * (scale * math.log2(math.e))) * valid for b in both]
    probs = [r * (1.0 / jnp.sum(r, axis=0, keepdims=True)) for r in raw]
    delta = [jnp.sum(p * g, axis=0, keepdims=True) for p, g in zip(probs, grad_probs)]
    low = [
        cat([(p * ((g - d) * scale)).astype(BF16), p.astype(BF16)], 0)
        for p, g, d in zip(probs, grad_probs, delta)
    ]
    for h, c in enumerate(cols):
        grads = dot(low[h], cat([q_ref[:, c], g_ref[:, c]], 1), ((1,), (0,)))
        chip, of_core, at = h * HEAD // (2 * group), h * HEAD // group % 2, h * HEAD % group
        first = lax.bitwise_xor(core, of_core) * 2 * group + at
        out_ref[chip, :, pl.ds(pl.multiple_of(first, HEAD), HEAD)] = grads[:src, :HEAD].astype(BF16)
        out_ref[chip, :, pl.ds(pl.multiple_of(first + group, HEAD), HEAD)] = grads[src:, HEAD:].astype(BF16)


def attention(place, lens, q, k, v, g, chips, group, first, count, earlier=None):
    tgt, src = q.shape[0], k.shape[0]
    some = 2
    wide = 2 * group * some
    begin = first // some

    def col(p, place, lens):
        return (0, begin + p)

    return pl.pallas_call(
        attention_kernel,
        grid_spec=pltpu.PrefetchScalarGridSpec(
            num_scalar_prefetch=2,
            grid=(count // some,),
            in_specs=[
                pl.BlockSpec((tgt, wide), col),
                pl.BlockSpec((src, wide), col),
                pl.BlockSpec((src, wide), col),
                pl.BlockSpec((tgt, wide), col),
            ]
            + ([] if earlier is None else [pl.BlockSpec(memory_space=pl.ANY)]),
            out_specs=pl.BlockSpec((some, src, 4 * group), lambda p, place, lens: (begin + p, 0, 0)),
        ),
        out_shape=jax.ShapeDtypeStruct((chips, src, 4 * group), BF16),
        input_output_aliases={} if earlier is None else {6: 0},
        compiler_params=pltpu.CompilerParams(vmem_limit_bytes=56 * MIB),
        cost_estimate=pl.CostEstimate(flops=350_000_000, bytes_accessed=4 * MIB, transcendentals=300_000),
        name="attention",
    )(place, lens, q, k, v, g, *([] if earlier is None else [earlier]))


def partial_kernel(kv_ref, kw_ref, vw_ref, okw_ref, ovw_ref, out_ref):
    w = kw_ref.shape[1]
    total = None
    for i, ref in enumerate((kw_ref, vw_ref, okw_ref, ovw_ref)):
        term = dot(kv_ref[:, i * w : (i + 1) * w], ref[...], ((1,), (1,)))
        total = term if total is None else total + term
    out_ref[...] = total.astype(BF16)


def encoder_partial(kv, kw, vw, okw, ovw):
    rows, feats = kv.shape
    width, w = kw.shape
    tile = 512
    spec = pl.BlockSpec((tile, w), lambda j: (j, 0))
    return pl.pallas_call(
        partial_kernel,
        grid=(width // tile,),
        in_specs=[pl.BlockSpec((rows, feats), lambda j: (0, 0)), spec, spec, spec, spec],
        out_specs=pl.BlockSpec((rows, tile), lambda j: (0, j)),
        out_shape=jax.ShapeDtypeStruct((rows, width), BF16),
        compiler_params=pltpu.CompilerParams(vmem_limit_bytes=56 * MIB),
        cost_estimate=pl.CostEstimate(
            flops=2 * rows * feats * width, bytes_accessed=16 * MIB, transcendentals=0
        ),
        name="encoder_partial",
    )(kv, kw, vw, okw, ovw)


def two_parts(x):
    high = x.astype(BF16)
    low = (x - high.astype(F32)).astype(BF16)
    return high, low


def update_kernel(z_shifts, y_shifts, spot, *refs):
    count = 2 * len(y_shifts)
    pieces, rest = refs[:count], refs[count:]
    kv_ref, okv_ref, key_ref, value_ref, lines, parts, gram, mix, result, sems = rest
    width = pieces[0].shape[1]
    inner = key_ref.shape[1]
    heads = inner // HEAD
    chunk = inner
    chunks = width // chunk

    row = lax.broadcasted_iota(jnp.int32, (HEAD, HEAD), 0)
    eye = (row == lax.broadcasted_iota(jnp.int32, (HEAD, HEAD), 1)).astype(F32)

    def prod(a, b):
        return dot(a, b, ((1,), (0,)), HIGHEST)

    def near_prod(a, b):
        left = jnp.concatenate(two_parts(a), axis=1)
        line = jnp.concatenate(two_parts(b), axis=1)
        full = dot(left, jnp.concatenate([line, line], axis=0), ((1,), (0,)))
        return full[:, :HEAD] + full[:, HEAD:]

    at = 0
    for ref in (kv_ref, okv_ref):
        for y in y_shifts:
            of_y = lax.rem(spot[2] + (4 - y), 4)
            some = jnp.concatenate(
                [
                    ref[lax.bitwise_xor(spot[0], x) * 4 + lax.rem(spot[1] + (4 - z), 4), of_y]
                    for z in z_shifts
                    for x in range(2)
                ],
                axis=0,
            )
            lines[:, at : at + some.shape[0]] = some.T
            at += some.shape[0]

    def lanes(i):
        return slice(i * chunk, (i + 1) * chunk)

    def sums(first, i):
        rows = jnp.concatenate([ref[:, lanes(i)] for ref in pieces], axis=0)
        total = dot(lines[first * HEAD : (first + heads) * HEAD], rows, ((1,), (0,)))
        for h in range(heads):
            both = jnp.concatenate(two_parts(total[h * HEAD : (h + 1) * HEAD]), axis=0)
            parts[first + h, :, lanes(i)] = both
            full = dot(both, both, ((1,), (1,)))
            term = (full[:HEAD, :HEAD] + full[HEAD:, HEAD:]) + (full[:HEAD, HEAD:] + full[HEAD:, :HEAD])
            gram[first + h] = gram[first + h] + term

    def start(first):
        for h in range(first, first + heads):
            whole = gram[h]
            trace = jnp.sum(jnp.sum(whole * eye, axis=1, keepdims=True), axis=0, keepdims=True)
            inverse = 1.0 / (jnp.sqrt(trace) + 1e-07)
            gram[h] = whole * inverse * inverse
            mix[h] = eye * (inverse * math.sqrt(width))

    def sweep(first, last):
        grams = [gram[first + h] for h in range(heads)]
        squares = [near_prod(a, a) for a in grams]
        steps = [LINEAR_COEFF * eye + (SQUARE_COEFF * a + CUBIC_COEFF * s) for a, s in zip(grams, squares)]
        mixes = [near_prod(mix[first + h], m) for h, m in enumerate(steps)]
        for h in range(heads):
            mix[first + h] = mixes[h]
        if not last:
            halves = [prod(a, m) for a, m in zip(grams, steps)]
            nexts = [prod(m, a) for a, m in zip(halves, steps)]
            for h in range(heads):
                gram[first + h] = nexts[h]

    def leave(first, i, ref):
        rows = lanes(i)
        place = 0 if first == 0 else 1
        return pltpu.make_async_copy(result.at[place, rows], ref.at[rows], sems.at[place, i])

    def finish(first, i, ref):
        place = 0 if first == 0 else 1
        for h in range(heads):
            line = jnp.concatenate(two_parts(mix[first + h]), axis=1)
            right = jnp.concatenate([line, line], axis=0)
            out = dot(parts[first + h, :, lanes(i)], right, ((0,), (0,)))
            result[place, lanes(i), h * HEAD : (h + 1) * HEAD] = out[:, :HEAD] + out[:, HEAD:]
        leave(first, i, ref).start()

    gram[...] = jnp.zeros_like(gram)

    for i in range(chunks):
        sums(0, i)
    start(0)
    for i in range(SWEEPS):
        sums(heads, i)
        sweep(0, i == SWEEPS - 1)
    start(heads)
    for i in range(SWEEPS):
        finish(0, i, key_ref)
        sweep(heads, i == SWEEPS - 1)
    for i in range(chunks):
        finish(heads, i, value_ref)
    for i in range(chunks):
        leave(0, i, key_ref).wait()
        leave(heads, i, value_ref).wait()


def updates(spot, z_shifts, y_shifts, pieces, kv, okv, inner):
    rows, width = pieces[0].shape
    blocks, size, block = kv.shape[:3]
    heads = 2 * inner // HEAD
    chunks = width // inner
    assert chunks == SWEEPS
    whole = pl.BlockSpec((rows, width), lambda i, spot: (0, 0))

    def half(at):
        return pl.BlockSpec((blocks, size, block, 2 * inner), lambda i, spot: (0, 0, 0, at))

    return pl.pallas_call(
        functools.partial(update_kernel, z_shifts, y_shifts),
        grid_spec=pltpu.PrefetchScalarGridSpec(
            num_scalar_prefetch=1,
            grid=(1,),
            in_specs=[whole] * len(pieces) + [half(0), half(1)],
            out_specs=[pl.BlockSpec(memory_space=pl.ANY)] * 2,
            scratch_shapes=[
                pltpu.VMEM((2 * inner, 2 * blocks * size * block), BF16),
                pltpu.VMEM((heads, 2 * HEAD, width), BF16),
                pltpu.VMEM((heads, HEAD, HEAD), F32),
                pltpu.VMEM((heads, HEAD, HEAD), F32),
                pltpu.VMEM((2, width, inner), F32),
                pltpu.SemaphoreType.DMA((2, chunks)),
            ],
        ),
        out_shape=[jax.ShapeDtypeStruct((width, inner), F32)] * 2,
        compiler_params=pltpu.CompilerParams(vmem_limit_bytes=56 * MIB),
        cost_estimate=pl.CostEstimate(
            flops=20_000_000_000, bytes_accessed=20 * MIB, transcendentals=0
        ),
        name="updates",
    )(spot, *pieces, kv, okv)


def ring(shift):
    return [(j, (j + shift) % 4) for j in range(4)]


def body(
    encoded, source_len, queries, saved_keys, saved_values, out_grad, key_weight, value_weight
):
    across = [(0, 1), (1, 0)]
    key_weight, value_weight = key_weight[0], value_weight[0]
    width, inner = key_weight.shape
    block = encoded.shape[1]

    place = lax.axis_index(("xl", "z", "c")).astype(jnp.int32).reshape(1)
    given = (queries[0, 0], saved_keys[0, 0], saved_values[0, 0], out_grad[0, 0])
    across_x = lax.ppermute(encoded[0], "xh", across)
    local = attention(place, source_len, *given, 8, inner, 0, 2)
    across_x, local = lax.optimization_barrier((across_x, local))
    low = lax.axis_index("xh") == 0
    pair = jnp.concatenate([jnp.where(low, encoded[0], across_x), jnp.where(low, across_x, encoded[0])], axis=0)
    next_x = lax.ppermute(pair, "xl", across)
    local = attention(place, source_len, *given, 8, inner, 2, 2, local)
    next_x, local = lax.optimization_barrier((next_x, local))
    pair = jnp.concatenate([pair, next_x], axis=0)
    z_shifts = (0, 2, 1, 3)
    along_z = [pair] + [lax.ppermute(pair, "z", ring(s)) for s in z_shifts[1:]]
    local = attention(place, source_len, *given, 8, inner, 4, 4, local)
    moved = lax.all_to_all(local, ("xl", "z"), split_axis=0, concat_axis=0, tiled=True)

    near = jnp.concatenate(along_z, axis=0)
    key_send, value_send, _ = lax.optimization_barrier((key_weight, value_weight, local))
    shifts = (0, 2, 1, 3)
    own_rows = [near] + [lax.ppermute(near, "y", ring(s)) for s in shifts[1:]]
    other_kw = lax.ppermute(key_send, "c", across)
    other_vw = lax.ppermute(value_send, "c", across)

    moved, own_rows[2], own_rows[3] = lax.optimization_barrier((moved, own_rows[2], own_rows[3]))
    rows = moved.reshape(8 * local.shape[1], 4 * inner)
    other_rows = [lax.ppermute(r, "c", across) for r in own_rows]
    other_moved = lax.ppermute(moved, "c", across)
    partial = encoder_partial(rows, key_weight, value_weight, other_kw, other_vw)
    terms = lax.all_to_all(
        partial, ("xl", "z", "y", "xh"), split_axis=0, concat_axis=0, tiled=True
    )

    spot = jnp.stack([lax.axis_index(a).astype(jnp.int32) for a in ("xl", "z", "y")])
    by_y = (8, 4, 2 * block, 4 * inner)
    key_update, value_update = updates(
        spot, z_shifts, shifts, own_rows + other_rows, moved.reshape(by_y), other_moved.reshape(by_y), inner
    )
    encoder_grad = jnp.sum(terms.reshape(64, block, width).astype(F32), axis=0)
    return encoder_grad[None], key_update[None], value_update[None]


def solution(mesh):
    fine = Mesh(mesh.devices.reshape(2, 4, 2, 4, 2), ("xl", "z", "c", "y", "xh"))
    dp, section = ("xl", "z", "c"), ("y", "xh")
    in_specs = (
        P(dp, section, None),
        P(),
        P(section, dp, None, None),
        P(section, dp, None, None),
        P(section, dp, None, None),
        P(section, dp, None, None),
        P(section, None, dp),
        P(section, None, dp),
    )
    out_specs = (P(dp, section, None), P(section, None, dp), P(section, None, dp))
    return jax.shard_map(body, mesh=fine, in_specs=in_specs, out_specs=out_specs, check_vma=False)
```
